32 devices in a mesh: group: 2 (over x), blk: 8 (over z, y), ulysses: 2 (over core).
Axes of the slice: x: 2, y: 2, z: 4, core: 2. Of those that a mesh axis runs over, the one named last changes fastest.
Arguments:
- query_int: bfloat16 [4096, 8192], P(('group', 'blk', 'ulysses')), parts along dimension 0, may hold values from -127 to 127, as said below
- key_int: bfloat16 [4096, 1024], P(('group', 'blk', 'ulysses')), parts along dimension 0, may hold values from -127 to 127, as said below
- values: bfloat16 [4096, 1024], P(('group', 'blk', 'ulysses')), parts along dimension 0, may hold values from -6 to 6
- query_scale: bfloat16 [32, 64], P(('group', 'blk')), parts along dimension 0, may hold values from 0.001 to 0.02
- key_scale: bfloat16 [32, 8], P('group'), parts along dimension 0, may hold values from 0.002 to 0.04
- verticals: int32 [16, 8], P('group'), parts along dimension 0, may hold values from 0 to 15, as said below
- slashes: int32 [16, 8], P('group'), parts along dimension 0, may hold values from 0 to 8, as said below
Outputs:
- attention: bfloat16 [4096, 8192], P(('group', 'blk', 'ulysses')), parts along dimension 0
The draws below stay inside these ranges and needn't reach their ends.
There are 2 independent parts, one for each index of `group`. The reference program is written for one: setup_inputs(seed, part) draws one part's arguments, and reference() takes and returns one part's arrays. A program takes and returns all parts, laid end to end along the dimension named above; each array names one. Nothing has to cross between parts.
Inputs may be any that keep to these rules, and one draw needn't show every extreme that they name: `query_int`: integer values. `key_int`: integer values. `verticals`: each row holds 8 distinct key blocks, block 0 among them. `slashes`: each row holds 8 distinct offsets, 0 among them.
All inputs are finite; a program needn't handle non-finite values.
Results may differ from the reference program's by a relative error of at most 0.0019.
Values may be sent and summed in bfloat16 or wider, within the bound.
No kernel may reach another device: no remote copies, remote signals or barrier semaphores. Data moves between devices by JAX's collectives and lax.ppermute only.
A program may use at most 128 MiB of HBM per device.

```python
import jax
import jax.numpy as jnp
from jax import lax

H = 64
KVH = 8
DH = 128
BLOCK = 128
BPD = 2
NV = 8
NSL = 8
SPAN = 4
QB = 16
SEQ = 2048


def integer_pair(key):
    keys_drawn = jax.random.randint(jax.random.fold_in(key, 101), (SEQ, KVH * DH), -127, 128)
    queries_drawn = jax.random.randint(jax.random.fold_in(key, 202), (SEQ, H * DH), -127, 128)
    return (queries_drawn.astype(jnp.float32), keys_drawn.astype(jnp.float32))


def draw_query_int(key, part):
    queries_drawn, keys_drawn = integer_pair(key)
    return queries_drawn.astype(jnp.bfloat16)


def draw_key_int(key, part):
    queries_drawn, keys_drawn = integer_pair(key)
    return keys_drawn.astype(jnp.bfloat16)


def log_between(key, shape, lower, upper):
    return jnp.exp(jax.random.uniform(key, shape, jnp.float32, jnp.log(lower), jnp.log(upper)))


def draw_query_scale(key, part):
    local_key = jax.random.fold_in(key, 303)
    drawn = log_between(local_key, (QB, H), 0.00101, 0.0199)
    return drawn.astype(jnp.bfloat16)


def draw_key_scale(key, part):
    local_key = jax.random.fold_in(key, 404)
    drawn = log_between(local_key, (QB, KVH), 0.00202, 0.0398)
    return drawn.astype(jnp.bfloat16)


def distinct_rows(key, tag, upper, picks):

    def one_row(row_index):
        order = jax.random.permutation(jax.random.fold_in(jax.random.fold_in(key, tag), row_index), upper - 1) + 1
        return jnp.concatenate([jnp.zeros((1,), jnp.int32), order[:picks - 1].astype(jnp.int32)])
    rows_drawn = jax.vmap(one_row)(jnp.arange(KVH))
    return rows_drawn.at[0, picks - 1].set(upper)


def draw_verticals(key, part):
    return distinct_rows(key, 505, QB - 1, NV)


def draw_slashes(key, part):
    return distinct_rows(key, 606, SPAN * BPD, NSL)


def levels(key, shape, shards, low, top_value):
    def one(dim, parts):
        steps = jax.random.uniform(jax.random.fold_in(jax.random.fold_in(key, 6), dim), (parts,), jnp.float32, low / len(shards), top_value / len(shards))
        return jnp.repeat(jnp.exp(steps), shape[dim] // parts).reshape((-1,) + (1,) * (len(shape) - dim - 1))

    level = one(*shards[0])
    for cut in shards[1:]:
        level = level * one(*cut)
    return level


def scatter_about(own_key, shape, scale, limit, cuts=(), kind=jnp.bfloat16):
    loudness = levels(own_key, shape, cuts, -0.22, 0.18) if cuts else 1.0
    values = jax.random.normal(own_key, shape, jnp.float32) * scale * loudness
    return jnp.minimum(jnp.maximum(values, -limit), limit).astype(kind)


def setup_inputs(seed: int = 0, part: int = 0) -> dict:
    arg_keys = jax.random.split(jax.random.key(seed), 8)
    own_keys = jax.random.split(jax.random.fold_in(arg_keys[7], part), 8)
    return {
        "query_int": draw_query_int(jax.random.fold_in(jax.random.fold_in(arg_keys[7], part), 71), part),
        "key_int": draw_key_int(jax.random.fold_in(jax.random.fold_in(arg_keys[7], part), 71), part),
        "values": scatter_about(own_keys[2], (SEQ, KVH * DH), 1.0, 6.0, ((0, 16),)),
        "query_scale": draw_query_scale(jax.random.fold_in(jax.random.fold_in(arg_keys[7], part), 71), part),
        "key_scale": draw_key_scale(jax.random.fold_in(jax.random.fold_in(arg_keys[7], part), 71), part),
        "verticals": draw_verticals(jax.random.fold_in(jax.random.fold_in(arg_keys[7], part), 71), part),
        "slashes": draw_slashes(jax.random.fold_in(jax.random.fold_in(arg_keys[7], part), 71), part),
    }


FLOOR_SCORE = -1e30


def block_table(verticals, slashes, first_block, block_count):
    blocks = first_block + jnp.arange(block_count, dtype=jnp.int32)
    slash_keys = blocks[:, None, None] - slashes[None, :, :]
    slash_live = slash_keys >= 0
    vert_keys = jnp.broadcast_to(verticals[None, :, :], (block_count,) + verticals.shape)
    clashes = jnp.any((vert_keys[:, :, :, None] == slash_keys[:, :, None, :]) & slash_live[:, :, None, :], axis=3)
    vert_live = (vert_keys <= blocks[:, None, None]) & jnp.logical_not(clashes)
    return (jnp.concatenate([vert_keys, slash_keys], axis=2), jnp.concatenate([vert_live, slash_live], axis=2), blocks)


def attend_block(query_block, query_scales, key_blocks, value_blocks, key_scales, live_slots, diagonal):
    dots = jnp.einsum("tgpd,gnsd->gptns", query_block.astype(jnp.float32), key_blocks.astype(jnp.float32))
    scores = dots * query_scales[:, :, None, None, None] * key_scales[:, None, None, :, None]
    width = query_block.shape[0]
    causal = jnp.arange(width)[None, :] <= jnp.arange(width)[:, None]
    allowed = live_slots[:, None, None, :, None] & (jnp.logical_not(diagonal)[:, None, None, :, None] | causal[None, None, :, None, :])
    masked = jnp.where(allowed, scores, FLOOR_SCORE)
    largest = jnp.max(masked, axis=(3, 4), keepdims=True)
    weights = jnp.where(allowed, jnp.exp(masked - largest), 0.0)
    totals = jnp.sum(weights, axis=(3, 4))
    probs = weights.astype(jnp.bfloat16)
    numer = jnp.einsum("gptns,gnsd->tgpd", probs.astype(jnp.float32), value_blocks.astype(jnp.float32))
    return (numer / jnp.transpose(totals, (2, 0, 1))[:, :, :, None]).astype(jnp.bfloat16)


def reference(query_int, key_int, values, query_scale, key_scale, verticals, slashes):
    per_group = H // KVH
    key_shaped = key_int.reshape(QB, BLOCK, KVH, DH)
    value_shaped = values.reshape(QB, BLOCK, KVH, DH)
    group_ids = jnp.arange(KVH, dtype=jnp.int32)

    def one_block(block_index):
        block_keys, live_slots, blocks = block_table(verticals, slashes, block_index, 1)
        clipped = jnp.clip(block_keys[0], 0, QB - 1).astype(jnp.int32)
        key_blocks = key_shaped[clipped, :, group_ids[:, None], :]
        value_blocks = value_shaped[clipped, :, group_ids[:, None], :]
        key_scales = key_scale[clipped, group_ids[:, None]].astype(jnp.float32)
        start_row = (block_index * BLOCK).astype(jnp.int32)
        query_block = lax.dynamic_slice_in_dim(query_int, start_row, BLOCK, 0).reshape(BLOCK, KVH, per_group, DH)
        query_scales = lax.dynamic_slice_in_dim(query_scale, block_index.astype(jnp.int32), 1, 0).astype(jnp.float32).reshape(KVH, per_group)
        diagonal = block_keys[0] == block_index
        return attend_block(query_block, query_scales, key_blocks, value_blocks, key_scales, live_slots[0], diagonal)

    outputs = lax.map(one_block, jnp.arange(QB, dtype=jnp.int32))
    return outputs.reshape(SEQ, H * DH)
```

```python
import functools

import jax
import jax.numpy as jnp
from jax import lax
from jax.experimental import pallas as pl
from jax.experimental.pallas import tpu as pltpu
from jax.sharding import PartitionSpec as P

DH = 128
FLOOR_SCORE = -1e30
LOG2E = 1.4426950408889634
NT = (((1,), (1,)), ((), ()))
F32 = jnp.float32
BF16 = jnp.bfloat16


def attend(count, diagonal, first, group, block, per_group, scale_at, keys_ref, values_ref, query_ref, state):
    most_ref, total_ref, sum_ref = state
    width = per_group * block
    base = pl.multiple_of(group * width, width)
    wide = pl.multiple_of(group * per_group * DH, per_group * DH)
    keys = keys_ref[0 : count * block, :]
    values = values_ref[:, 0 : count * block]

    def dots_of(head):
        query = query_ref[:, pl.ds(wide + head * DH, DH)]
        return lax.dot_general(keys, query, NT, preferred_element_type=F32)

    def weigh(head, dots):
        here = pl.ds(base + head * block, block)
        parts = []
        for slot in range(count):
            part = dots[slot * block : (slot + 1) * block] * scale_at(slot, head)
            if diagonal and slot == 0:
                key_at = lax.broadcasted_iota(jnp.int32, part.shape, 0)
                query_at = lax.broadcasted_iota(jnp.int32, part.shape, 1)
                part = jnp.where(key_at <= query_at, part, FLOOR_SCORE)
            parts.append(part)
        most = functools.reduce(jnp.maximum, [jnp.max(part, axis=0, keepdims=True) for part in parts])
        shrink = None
        if not first:
            before = most_ref[:, here]
            most = jnp.maximum(most, before)
            shrink = jnp.exp2(before - most)
        weights = [jnp.exp2(part - most) for part in parts]
        total = functools.reduce(jnp.add, [jnp.sum(part, axis=0, keepdims=True) for part in weights])
        if not first:
            total = total + total_ref[:, here] * shrink
        most_ref[:, here] = most
        total_ref[:, here] = total
        return jnp.concatenate([part.astype(BF16) for part in weights], axis=0), shrink

    def gather(head, probs, shrink):
        here = pl.ds(base + head * block, block)
        add = jnp.dot(values, probs, preferred_element_type=F32)
        sum_ref[:, here] = add if first else sum_ref[:, here] * shrink + add

    dots = dots_of(0)
    pending = None
    for head in range(per_group):
        ahead = dots_of(head + 1) if head + 1 < per_group else None
        if pending is not None:
            gather(*pending)
        pending = (head,) + weigh(head, dots)
        dots = ahead
    gather(*pending)


def chunk_kernel(pieces, first, last, groups, per_group, block, *refs):
    scale_ref, live_ref, query_ref = refs[:3]
    piece_refs = refs[3 : 3 + pieces]
    rest = refs[3 + pieces :]
    if first:
        state, rest = rest[:3], rest[3:]
    else:
        rest = rest[3:]
        state, rest = rest[:3], rest[3:]
    if last:
        out_ref, rest = rest[0], rest[1:]
    keys_ref, values_ref, slot_ref = rest
    width = per_group * block

    @pl.loop(0, groups)
    def _(group):
        count = jnp.int32(0)
        column = pl.ds(pl.multiple_of(group * DH, DH), DH)
        for piece in range(pieces):
            live = live_ref[piece, group]

            @pl.when(live > 0)
            def _(piece=piece, count=count):
                at = pl.ds(pl.multiple_of(count * block, block), block)
                keys_ref[at, :] = piece_refs[piece][0:block, column]
                values_ref[:, at] = piece_refs[piece][block : 2 * block, column].T
                slot_ref[count] = piece

            count = count + live

        def scale_at(slot, head):
            return scale_ref[slot_ref[slot], group * per_group + head]

        for many in range(1, pieces + 1):

            @pl.when(count == many)
            def _(many=many):
                attend(
                    many, first, first, group, block, per_group, scale_at, keys_ref, values_ref, query_ref, state
                )

        if last:
            for head in range(per_group):
                here = pl.ds(pl.multiple_of(group * width, width) + head * block, block)
                done = state[2][:, here] / state[1][:, here]
                out_ref[:, pl.ds(pl.multiple_of(group * per_group * DH, DH) + head * DH, DH)] = done.T.astype(BF16)


def attend_chunk(query, pieces, scales, live, state, last):
    rows, features = query.shape
    heads = scales.shape[1]
    groups = live.shape[1]
    block = rows
    first = state is None
    count = len(pieces)
    kernel = functools.partial(chunk_kernel, count, first, last, groups, heads // groups, block)
    smem = pl.BlockSpec(memory_space=pltpu.SMEM)
    vmem = pl.BlockSpec(memory_space=pltpu.VMEM)
    state_shape = [
        jax.ShapeDtypeStruct((1, heads * block), F32),
        jax.ShapeDtypeStruct((1, heads * block), F32),
        jax.ShapeDtypeStruct((DH, heads * block), F32),
    ]
    out_shape = state_shape + ([jax.ShapeDtypeStruct(query.shape, BF16)] if last else [])
    operands = [scales, live, query, *pieces] + ([] if first else list(state))
    flops = 4 * count * block * block * heads * DH
    outs = pl.pallas_call(
        kernel,
        in_specs=[smem, smem] + [vmem] * (len(operands) - 2),
        out_specs=[vmem] * len(out_shape),
        out_shape=out_shape,
        scratch_shapes=[
            pltpu.VMEM((count * block, DH), BF16),
            pltpu.VMEM((DH, count * block), BF16),
            pltpu.SMEM((count,), jnp.int32),
        ],
        input_output_aliases={} if first else {3 + count + i: i for i in range(3)},
        compiler_params=pltpu.CompilerParams(vmem_limit_bytes=24 * 2**20),
        cost_estimate=pl.CostEstimate(flops=flops, bytes_accessed=0, transcendentals=0),
    )(*operands)
    return outs[3] if last else outs


def local(spans, cores, query_int, key_int, values, query_scale, key_scale, verticals, slashes):
    block = query_int.shape[0]
    heads = query_int.shape[1] // DH
    groups = key_int.shape[1] // DH
    pair = 2 if spans % 2 == 0 else 1
    lines = spans // pair
    span = lax.axis_index("blk")
    core = lax.axis_index("ulysses")
    line, side = span // pair, span % pair
    here = span * cores + core

    own = jnp.concatenate([key_int, values], axis=0)
    climb = [(s, s + pair) for s in range(spans - pair)]
    swap = [(s, s ^ 1) for s in range(spans)]
    turn = [(c, (c + 1) % cores) for c in range(cores)]

    def both(piece, origin):
        found = [(piece, origin(core))]
        for step in range(1, cores):
            piece = lax.ppermute(piece, "ulysses", turn)
            found.append((piece, origin((core - step) % cores)))
        return found

    chunks = [both(own, lambda c: span * cores + c)]
    climbed = own
    for step in range(lines):
        fresh = []
        crossed = lax.ppermute(climbed, "blk", swap) if pair == 2 else None
        behind = line - step
        if step + 1 < lines:
            climbed = lax.ppermute(climbed, "blk", climb)
            before = behind - 1
            fresh += both(climbed, lambda c: jnp.where(before >= 0, (before * pair + side) * cores + c, here + 1))
        if pair == 2:
            fresh += both(crossed, lambda c: jnp.where(behind >= 0, (behind * pair + 1 - side) * cores + c, here + 1))
        chunks.append(fresh)

    query_scales = lax.dynamic_slice_in_dim(query_scale, core, 1, 0).astype(F32)
    state = None
    for index, chunk in enumerate(chunks):
        places = jnp.stack([place for _, place in chunk]).astype(jnp.int32)
        seen = jnp.any(places[:, None, None] == here - slashes[None], axis=2) | jnp.any(
            places[:, None, None] == verticals[None], axis=2
        )
        live = (seen & (places <= here)[:, None]).astype(jnp.int32)
        key_scales = key_scale[jnp.minimum(places, key_scale.shape[0] - 1)].astype(F32)
        scales = query_scales * jnp.repeat(key_scales, heads // groups, axis=1) * LOG2E
        state = attend_chunk(
            query_int, [piece for piece, _ in chunk], scales, live, state, index + 1 == len(chunks)
        )
    return state


def solution(mesh):
    rows = P(("group", "blk", "ulysses"), None)
    in_specs = (rows, rows, rows, P(("group", "blk"), None), P("group", None), P("group", None), P("group", None))
    run = functools.partial(local, mesh.shape["blk"], mesh.shape["ulysses"])
    return jax.shard_map(run, mesh=mesh, in_specs=in_specs, out_specs=rows, check_vma=False)
```

```python
import functools

import jax
import jax.numpy as jnp
from jax import lax
from jax.experimental import pallas as pl
from jax.experimental.pallas import tpu as pltpu
from jax.sharding import PartitionSpec as P

DH = 128
FLOOR_SCORE = -1e30
LOG2E = 1.4426950408889634
NT = (((1,), (1,)), ((), ()))
F32 = jnp.float32
BF16 = jnp.bfloat16


def attend(count, diagonal, first, group, block, per_group, scale_at, keys_ref, values_ref, query_ref, state):
    most_ref, total_ref, sum_ref = state
    width = per_group * block
    base = pl.multiple_of(group * width, width)
    wide = pl.multiple_of(group * per_group * DH, per_group * DH)
    keys = keys_ref[0 : count * block, :]
    values = values_ref[:, 0 : count * block]

    def dots_of(head):
        query = query_ref[:, pl.ds(wide + head * DH, DH)]
        return lax.dot_general(keys, query, NT, preferred_element_type=F32)

    def weigh(head, dots):
        here = pl.ds(base + head * block, block)
        parts = []
        for slot in range(count):
            part = dots[slot * block : (slot + 1) * block] * scale_at(slot, head)
            if diagonal and slot == 0:
                key_at = lax.broadcasted_iota(jnp.int32, part.shape, 0)
                query_at = lax.broadcasted_iota(jnp.int32, part.shape, 1)
                part = jnp.where(key_at <= query_at, part, FLOOR_SCORE)
            parts.append(part)
        most = functools.reduce(jnp.maximum, [jnp.max(part, axis=0, keepdims=True) for part in parts])
        shrink = None
        if not first:
            before = most_ref[:, here]
            most = jnp.maximum(most, before)
            shrink = jnp.exp2(before - most)
        weights = [jnp.exp2(part - most) for part in parts]
        total = functools.reduce(jnp.add, [jnp.sum(part, axis=0, keepdims=True) for part in weights])
        if not first:
            total = total + total_ref[:, here] * shrink
        most_ref[:, here] = most
        total_ref[:, here] = total
        return jnp.concatenate([part.astype(BF16) for part in weights], axis=0), shrink

    def gather(head, probs, shrink):
        here = pl.ds(base + head * block, block)
        add = jnp.dot(values, probs, preferred_element_type=F32)
        sum_ref[:, here] = add if first else sum_ref[:, here] * shrink + add

    dots = dots_of(0)
    pending = None
    for head in range(per_group):
        ahead = dots_of(head + 1) if head + 1 < per_group else None
        if pending is not None:
            gather(*pending)
        pending = (head,) + weigh(head, dots)
        dots = ahead
    gather(*pending)


def chunk_kernel(pieces, first, last, groups, per_group, block, *refs):
    scale_ref, live_ref, query_ref = refs[:3]
    piece_refs = refs[3 : 3 + pieces]
    rest = refs[3 + pieces :]
    if first:
        state, rest = rest[:3], rest[3:]
    else:
        rest = rest[3:]
        state, rest = rest[:3], rest[3:]
    if last:
        out_ref, rest = rest[0], rest[1:]
    keys_ref, values_ref, slot_ref = rest
    width = per_group * block

    @pl.loop(0, groups)
    def _(group):
        count = jnp.int32(0)
        column = pl.ds(pl.multiple_of(group * DH, DH), DH)
        for piece in range(pieces):
            live = live_ref[piece, group]

            @pl.when(live > 0)
            def _(piece=piece, count=count):
                at = pl.ds(pl.multiple_of(count * block, block), block)
                keys_ref[at, :] = piece_refs[piece][0:block, column]
                values_ref[:, at] = piece_refs[piece][block : 2 * block, column].T
                slot_ref[count] = piece

            count = count + live

        def scale_at(slot, head):
            return scale_ref[slot_ref[slot], group * per_group + head]

        for many in range(1, pieces + 1):

            @pl.when(count == many)
            def _(many=many):
                attend(
                    many, first, first, group, block, per_group, scale_at, keys_ref, values_ref, query_ref, state
                )

        if last:
            for head in range(per_group):
                here = pl.ds(pl.multiple_of(group * width, width) + head * block, block)
                done = state[2][:, here] / state[1][:, here]
                out_ref[:, pl.ds(pl.multiple_of(group * per_group * DH, DH) + head * DH, DH)] = done.T.astype(BF16)


def attend_chunk(query, pieces, scales, live, state, last):
    rows, features = query.shape
    heads = scales.shape[1]
    groups = live.shape[1]
    block = rows
    first = state is None
    count = len(pieces)
    kernel = functools.partial(chunk_kernel, count, first, last, groups, heads // groups, block)
    smem = pl.BlockSpec(memory_space=pltpu.SMEM)
    vmem = pl.BlockSpec(memory_space=pltpu.VMEM)
    state_shape = [
        jax.ShapeDtypeStruct((1, heads * block), F32),
        jax.ShapeDtypeStruct((1, heads * block), F32),
        jax.ShapeDtypeStruct((DH, heads * block), F32),
    ]
    out_shape = state_shape + ([jax.ShapeDtypeStruct(query.shape, BF16)] if last else [])
    operands = [scales, live, query, *pieces] + ([] if first else list(state))
    flops = 4 * count * block * block * heads * DH
    outs = pl.pallas_call(
        kernel,
        in_specs=[smem, smem] + [vmem] * (len(operands) - 2),
        out_specs=[vmem] * len(out_shape),
        out_shape=out_shape,
        scratch_shapes=[
            pltpu.VMEM((count * block, DH), BF16),
            pltpu.VMEM((DH, count * block), BF16),
            pltpu.SMEM((count,), jnp.int32),
        ],
        input_output_aliases={} if first else {3 + count + i: i for i in range(3)},
        compiler_params=pltpu.CompilerParams(vmem_limit_bytes=24 * 2**20),
        cost_estimate=pl.CostEstimate(flops=flops, bytes_accessed=0, transcendentals=0),
    )(*operands)
    return outs[3] if last else outs


def local(spans, cores, query_int, key_int, values, query_scale, key_scale, verticals, slashes):
    block = query_int.shape[0]
    heads = query_int.shape[1] // DH
    groups = key_int.shape[1] // DH
    pair = 2 if spans % 2 == 0 else 1
    lines = spans // pair
    span = lax.axis_index("blk")
    core = lax.axis_index("ulysses")
    line, side = span // pair, span % pair
    here = span * cores + core

    own = jnp.concatenate([key_int, values], axis=0)
    climb = [(s, s + pair) for s in range(spans - pair)]
    swap = [(s, s ^ 1) for s in range(spans)]
    turn = [(c, (c + 1) % cores) for c in range(cores)]

    def both(piece, origin):
        found = [(piece, origin(core))]
        for step in range(1, cores):
            piece = lax.ppermute(piece, "ulysses", turn)
            found.append((piece, origin((core - step) % cores)))
        return found

    query_scales = lax.dynamic_slice_in_dim(query_scale, core, 1, 0).astype(F32)

    def table(places):
        places = jnp.stack(places).astype(jnp.int32)
        seen = jnp.any(places[:, None, None] == here - slashes[None], axis=2) | jnp.any(
            places[:, None, None] == verticals[None], axis=2
        )
        live = (seen & (places <= here)[:, None]).astype(jnp.int32)
        key_scales = key_scale[jnp.minimum(places, key_scale.shape[0] - 1)].astype(F32)
        return query_scales * jnp.repeat(key_scales, heads // groups, axis=1) * LOG2E, live

    climbed, crossed, state = own, None, None
    for step in range(lines + (pair == 2)):
        behind = line - step
        fresh = []
        arrived = []
        if step < lines:
            arrived.append((climbed, behind, side))
        if crossed is not None:
            arrived.append((crossed, behind + 1, 1 - side))
        sent = climbed
        crossed = lax.ppermute(sent, "blk", swap) if pair == 2 and step < lines else None
        climbed = lax.ppermute(sent, "blk", climb) if step + 1 < lines else None
        for piece, from_line, from_side in arrived:
            fresh += both(
                piece,
                lambda c: jnp.where(from_line >= 0, (from_line * pair + from_side) * cores + c, here + 1),
            )
        scales, live = table([place for _, place in fresh])
        last = step + 1 == lines + (pair == 2)
        state = attend_chunk(query_int, [piece for piece, _ in fresh], scales, live, state, last)
        if not last:
            climbed, crossed, state = lax.optimization_barrier((climbed, crossed, state))
    return state


def solution(mesh):
    rows = P(("group", "blk", "ulysses"), None)
    in_specs = (rows, rows, rows, P(("group", "blk"), None), P("group", None), P("group", None), P("group", None))
    run = functools.partial(local, mesh.shape["blk"], mesh.shape["ulysses"])
    return jax.shard_map(run, mesh=mesh, in_specs=in_specs, out_specs=rows, check_vma=False)
```

```python
import functools

import jax
import jax.numpy as jnp
from jax import lax
from jax.experimental import pallas as pl
from jax.experimental.pallas import tpu as pltpu
from jax.sharding import PartitionSpec as P

DH = 128
FLOOR_SCORE = -1e30
LOG2E = 1.4426950408889634
NT = (((1,), (1,)), ((), ()))
F32 = jnp.float32
BF16 = jnp.bfloat16
VMEM_LIMIT = 16 * 2**20


def along_rows(combine, parts):
    rows = [part[at : at + 8] for part in parts for at in range(0, part.shape[0], 8)]
    lanes = rows[:4]
    for at, row in enumerate(rows[4:]):
        lanes[at % 4] = combine(lanes[at % 4], row)
    return functools.reduce(combine, lanes)


def attend(count, diagonal, first, group, block, per_group, scale_at, keys_ref, values_ref, query_ref, state):
    most_ref, total_ref, sum_ref = state
    base = pl.multiple_of(group * per_group * block, per_group * block)
    keys = keys_ref[0 : count * block, :]
    values = values_ref[:, 0 : count * block]

    def dots_of(head):
        return lax.dot_general(keys, query_ref[:, head * DH : (head + 1) * DH], NT, preferred_element_type=F32)

    def weigh(head, dots):
        here = pl.ds(base + head * block, block)
        parts = []
        for slot in range(count):
            part = dots[slot * block : (slot + 1) * block] * scale_at(slot, head)
            if diagonal and slot == 0:
                key_at = lax.broadcasted_iota(jnp.int32, part.shape, 0)
                query_at = lax.broadcasted_iota(jnp.int32, part.shape, 1)
                part = jnp.where(key_at <= query_at, part, FLOOR_SCORE)
            parts.append(part)
        most = jnp.max(along_rows(jnp.maximum, parts), axis=0, keepdims=True)
        shrink = None
        if not first:
            old = most_ref[:, here]
            most = jnp.maximum(most, old)
            shrink = jnp.exp2(old - most)
        weights = [jnp.exp2(part - most) for part in parts]
        total = jnp.sum(along_rows(jnp.add, weights), axis=0, keepdims=True)
        if not first:
            total = total + total_ref[:, here] * shrink
        most_ref[:, here] = most
        total_ref[:, here] = total
        return jnp.concatenate([part.astype(BF16) for part in weights], axis=0), shrink

    def gather(head, probs, shrink):
        here = pl.ds(base + head * block, block)
        add = jnp.dot(values, probs, preferred_element_type=F32)
        sum_ref[:, here] = add if first else sum_ref[:, here] * shrink + add

    dots = dots_of(0)
    pending = None
    for head in range(per_group):
        ahead = dots_of(head + 1) if head + 1 < per_group else None
        if pending is not None:
            gather(*pending)
        pending = (head,) + weigh(head, dots)
        dots = ahead
    gather(*pending)


def stack_kernel(top_ref, low_ref, out_ref, sems):
    rows = top_ref.shape[0]
    top = pltpu.make_async_copy(top_ref, out_ref.at[0:rows], sems.at[0])
    low = pltpu.make_async_copy(low_ref, out_ref.at[rows : 2 * rows], sems.at[1])
    top.start()
    low.start()
    top.wait()
    low.wait()


def stack(top, low):
    hbm = pl.BlockSpec(memory_space=pl.ANY)
    pinned = [pltpu.with_memory_space_constraint(array, pltpu.HBM) for array in (top, low)]
    return pl.pallas_call(
        stack_kernel,
        in_specs=[hbm, hbm],
        out_specs=pl.BlockSpec(memory_space=pltpu.VMEM),
        out_shape=jax.ShapeDtypeStruct((2 * top.shape[0], top.shape[1]), top.dtype),
        scratch_shapes=[pltpu.SemaphoreType.DMA((2,))],
        compiler_params=pltpu.CompilerParams(vmem_limit_bytes=VMEM_LIMIT),
    )(*pinned)


def live_at(group, place, here, table_ref, groups, width):
    seen = jnp.int32(0)
    back = here - place
    for index in range(width):
        seen = seen | (table_ref[1 + group * width + index] == place).astype(jnp.int32)
        seen = seen | (table_ref[1 + (groups + group) * width + index] == back).astype(jnp.int32)
    return jnp.where((place >= 0) & (back >= 0), seen, 0)


def chunk_kernel(origins, first, last, groups, per_group, block, table_width, heads, *refs):
    pieces = len(origins)
    table_ref, scale_ref, query_hbm = refs[:3]
    piece_refs = refs[3 : 3 + pieces]
    rest = refs[3 + pieces :]
    if not first:
        rest = rest[3:]
    state, rest = rest[:3], rest[3:]
    if last:
        out_hbm, rest = rest[0], rest[1:]
    query_ref, keys_ref, raw_ref, values_ref, slot_ref, count_ref, sems, out_ref, out_sems = rest
    width = per_group * block
    wide = per_group * DH
    here = table_ref[0]
    places = [origin(here) for origin in origins]

    def query_copy(group, buffer):
        columns = pl.ds(pl.multiple_of(group * wide, wide), wide)
        return pltpu.make_async_copy(query_hbm.at[:, columns], query_ref.at[buffer], sems.at[0, buffer])

    def tile_copies(piece, group, buffer, at):
        column = pl.ds(pl.multiple_of(group * DH, DH), DH)
        rows = pl.ds(pl.multiple_of(at * block, block), block)
        source = piece_refs[piece]
        return (
            pltpu.make_async_copy(source.at[0:block, column], keys_ref.at[buffer, rows], sems.at[1, buffer]),
            pltpu.make_async_copy(source.at[block : 2 * block, column], raw_ref.at[buffer, rows], sems.at[2, buffer]),
        )

    def fetch(group, buffer):
        query_copy(group, buffer).start()
        count = jnp.int32(0)
        for piece, place in enumerate(places):
            live = live_at(group, place, here, table_ref, groups, table_width)

            @pl.when(live > 0)
            def _(piece=piece, count=count, place=place):
                for copy in tile_copies(piece, group, buffer, count):
                    copy.start()
                slot_ref[buffer, count] = place

            count = count + live
        count_ref[buffer] = count

    def out_copy(group, buffer):
        columns = pl.ds(pl.multiple_of(group * wide, wide), wide)
        return pltpu.make_async_copy(out_ref.at[buffer], out_hbm.at[:, columns], out_sems.at[buffer])

    fetch(0, 0)

    @pl.loop(0, groups)
    def _(group):
        buffer = lax.rem(group, 2)

        @pl.when(group + 1 < groups)
        def _():
            fetch(group + 1, 1 - buffer)

        query_copy(group, buffer).wait()
        count = count_ref[buffer]
        for at in range(pieces):

            @pl.when(at < count)
            def _(at=at):
                for copy in tile_copies(0, group, buffer, at):
                    copy.wait()

        def scale_at(slot, head):
            key_scale = scale_ref[heads + slot_ref[buffer, slot] * groups + group]
            return scale_ref[group * per_group + head] * key_scale * LOG2E

        for many in range(1, pieces + 1):

            @pl.when(count == many)
            def _(many=many):
                for at in range(many):
                    values_ref[:, at * block : (at + 1) * block] = raw_ref[buffer, at * block : (at + 1) * block].T
                attend(
                    many, first, first, group, block, per_group, scale_at, keys_ref.at[buffer], values_ref,
                    query_ref.at[buffer], state,
                )

        if last:

            @pl.when(group >= 2)
            def _():
                out_copy(group - 2, buffer).wait()

            for head in range(per_group):
                at = pl.ds(pl.multiple_of(group * width, width) + head * block, block)
                done = state[2][:, at] * (1.0 / state[1][:, at])
                out_ref[buffer, :, head * DH : (head + 1) * DH] = done.T.astype(BF16)
            out_copy(group, buffer).start()

    if last:
        for group in range(max(0, groups - 2), groups):
            out_copy(group, group % 2).wait()


def attend_chunk(table, scales, query, pieces, origins, state, last, groups, table_width):
    rows, features = query.shape
    heads = features // DH
    per_group = heads // groups
    block = rows
    first = state is None
    count = len(pieces)
    kernel = functools.partial(chunk_kernel, origins, first, last, groups, per_group, block, table_width, heads)
    smem = pl.BlockSpec(memory_space=pltpu.SMEM)
    vmem = pl.BlockSpec(memory_space=pltpu.VMEM)
    hbm = pl.BlockSpec(memory_space=pl.ANY)
    state_shape = [
        jax.ShapeDtypeStruct((1, heads * block), F32),
        jax.ShapeDtypeStruct((1, heads * block), F32),
        jax.ShapeDtypeStruct((DH, heads * block), F32),
    ]
    outs = pl.pallas_call(
        kernel,
        in_specs=[smem] * 2 + [hbm] * (1 + count) + ([] if first else [vmem] * 3),
        out_specs=[vmem] * 3 + ([hbm] if last else []),
        out_shape=state_shape + ([jax.ShapeDtypeStruct(query.shape, BF16)] if last else []),
        scratch_shapes=[
            pltpu.VMEM((2, block, per_group * DH), BF16),
            pltpu.VMEM((2, count * block, DH), BF16),
            pltpu.VMEM((2, count * block, DH), BF16),
            pltpu.VMEM((DH, count * block), BF16),
            pltpu.SMEM((2, count), jnp.int32),
            pltpu.SMEM((2,), jnp.int32),
            pltpu.SemaphoreType.DMA((3, 2)),
            pltpu.VMEM((2, block, per_group * DH), BF16),
            pltpu.SemaphoreType.DMA((2,)),
        ],
        input_output_aliases={} if first else {3 + count + i: i for i in range(3)},
        compiler_params=pltpu.CompilerParams(vmem_limit_bytes=VMEM_LIMIT),
        cost_estimate=pl.CostEstimate(flops=1, bytes_accessed=0, transcendentals=0),
    )(table, scales, query, *pieces, *(() if first else state))
    return outs[3] if last else outs


def local(spans, cores, query_int, key_int, values, query_scale, key_scale, verticals, slashes):
    pair = 2 if spans % 2 == 0 else 1
    lines = spans // pair
    span = lax.axis_index("blk")
    core = lax.axis_index("ulysses")
    here = span * cores + core

    own = stack(key_int, values)
    swap = [(s, s ^ 1) for s in range(spans)]
    turn = [(c, (c + 1) % cores) for c in range(cores)]
    climb = [(s, s + pair) for s in range(spans - pair)]
    groups, table_width = verticals.shape
    table = jnp.concatenate([here[None].astype(jnp.int32), verticals.reshape(-1), slashes.reshape(-1)])
    query_scales = lax.dynamic_slice_in_dim(query_scale, core, 1, 0)
    scales = jnp.concatenate([query_scales.reshape(-1), key_scale.reshape(-1)]).astype(F32)

    def both(piece, back, other):
        found = []
        for step in range(cores):
            if step:
                piece = lax.ppermute(piece, "ulysses", turn)

            def origin(at, step=step):
                at_core, at_span = at % cores, at // cores
                at_line, at_side = at_span // pair - back, at_span % pair
                if other:
                    at_side = pair - 1 - at_side
                place = (at_line * pair + at_side) * cores + (at_core + cores - step) % cores
                return jnp.where(at_line >= 0, place, -1)

            found.append((piece, origin))
        return found

    climbed, crossed, state = own, None, None
    steps = lines + (pair == 2)
    for step in range(steps):
        fresh = []
        sent, arrived = climbed, crossed
        climbed = lax.ppermute(sent, "blk", climb) if step + 1 < lines else None
        crossed = lax.ppermute(sent, "blk", swap) if pair == 2 and sent is not None else None
        if sent is not None:
            fresh += both(sent, step, False)
        if arrived is not None:
            fresh += both(arrived, step - 1, True)
        last = step + 1 == steps
        pieces, origins = zip(*fresh)
        state = attend_chunk(table, scales, query_int, pieces, origins, state, last, groups, table_width)
        if not last:
            climbed, crossed, state = lax.optimization_barrier((climbed, crossed, state))
    return state


def solution(mesh):
    rows = P(("group", "blk", "ulysses"), None)
    in_specs = (rows, rows, rows, P(("group", "blk"), None), P("group", None), P("group", None), P("group", None))
    run = functools.partial(local, mesh.shape["blk"], mesh.shape["ulysses"])
    return jax.shard_map(run, mesh=mesh, in_specs=in_specs, out_specs=rows, check_vma=False)
```

```python
import functools

import jax
import jax.numpy as jnp
from jax import lax
from jax.experimental import pallas as pl
from jax.experimental.pallas import tpu as pltpu
from jax.sharding import PartitionSpec as P

DH = 128
FLOOR_SCORE = -1e30
LOG2E = 1.4426950408889634
NT = (((1,), (1,)), ((), ()))
F32 = jnp.float32
BF16 = jnp.bfloat16
VMEM_LIMIT = 16 * 2**20
ANYWHERE = pl.BlockSpec(memory_space=pl.ANY)
IN_VMEM = pl.BlockSpec(memory_space=pltpu.VMEM)
PARAMS = pltpu.CompilerParams(vmem_limit_bytes=VMEM_LIMIT)


def along_rows(combine, parts):
    rows = [part[at : at + 8] for part in parts for at in range(0, part.shape[0], 8)]
    lanes = rows[:4]
    for at, row in enumerate(rows[4:]):
        lanes[at % 4] = combine(lanes[at % 4], row)
    return functools.reduce(combine, lanes)


def attend(count, diagonal, block, per_group, scale_at, keys, values, query_ref, before, after, finish):
    abreast = 2 if count == 1 and per_group % 2 == 0 else 1

    def dots_of(head):
        queries = [query_ref[:, at * DH : (at + 1) * DH] for at in range(head, head + abreast)]
        return lax.dot_general(keys, jnp.concatenate(queries, axis=0), NT, preferred_element_type=F32)

    def weigh(head, dots):
        probs, shrinks, totals = [], [], []
        for at in range(abreast):
            parts = []
            for slot in range(count):
                part = dots[slot * block : (slot + 1) * block, at * block : (at + 1) * block]
                part = part * scale_at(slot, head + at)
                if diagonal and slot == 0:
                    key_at = lax.broadcasted_iota(jnp.int32, part.shape, 0)
                    query_at = lax.broadcasted_iota(jnp.int32, part.shape, 1)
                    part = jnp.where(key_at <= query_at, part, FLOOR_SCORE)
                parts.append(part)
            most = jnp.max(along_rows(jnp.maximum, parts), axis=0, keepdims=True)
            if before is not None:
                there = pl.ds(before[1] + (head + at) * block, block)
                old = before[0][0][:, there]
                most = jnp.maximum(most, old)
                shrinks.append(jnp.exp2(old - most))
            weights = [jnp.exp2(part - most) for part in parts]
            total = jnp.sum(along_rows(jnp.add, weights), axis=0, keepdims=True)
            if before is not None:
                total = total + before[0][1][:, there] * shrinks[-1]
            if after is not None:
                here = pl.ds(after[1] + (head + at) * block, block)
                after[0][0][:, here] = most
                after[0][1][:, here] = total
            totals.append(total)
            probs.append(jnp.concatenate([part.astype(BF16) for part in weights], axis=0))
        shrink = None if before is None else jnp.concatenate(shrinks, axis=1)
        return jnp.concatenate(probs, axis=1), shrink, jnp.concatenate(totals, axis=1)

    def gather(head, probs, shrink, total):
        add = jnp.dot(values, probs, preferred_element_type=F32)
        if before is not None:
            add = before[0][2][:, pl.ds(before[1] + head * block, abreast * block)] * shrink + add
        if finish is None:
            after[0][2][:, pl.ds(after[1] + head * block, abreast * block)] = add
            return
        for at in range(abreast):
            part = slice(at * block, (at + 1) * block)
            finish(head + at, add[:, part], total[:, part])

    dots = dots_of(0)
    pending = None
    for head in range(0, per_group, abreast):
        ahead = dots_of(head + abreast) if head + abreast < per_group else None
        if pending is not None:
            gather(*pending)
        pending = (head,) + weigh(head, dots)
        dots = ahead
    gather(*pending)


def run_copies(copies):
    for copy in copies:
        copy.start()
    for copy in copies:
        copy.wait()


def deal_kernel(cores, key_ref, value_ref, *rest):
    shares, sems = rest[:-1], rest[-1]
    rows, columns = key_ref.shape[0], key_ref.shape[1] // cores
    core = lax.axis_index("ulysses")
    copies = []
    for step, share in enumerate(shares):
        part = pl.ds(pl.multiple_of(lax.rem(core + cores - step, cores) * columns, columns), columns)
        copies.append(pltpu.make_async_copy(key_ref.at[:, part], share.at[0:rows], sems.at[step, 0]))
        copies.append(pltpu.make_async_copy(value_ref.at[:, part], share.at[rows : 2 * rows], sems.at[step, 1]))
    run_copies(copies)


def deal(cores, key_int, values):
    rows, columns = key_int.shape
    pinned = [pltpu.with_memory_space_constraint(array, pltpu.HBM) for array in (key_int, values)]
    return pl.pallas_call(
        functools.partial(deal_kernel, cores),
        in_specs=[ANYWHERE] * 2,
        out_specs=[IN_VMEM] * cores,
        out_shape=[jax.ShapeDtypeStruct((2 * rows, columns // cores), key_int.dtype)] * cores,
        scratch_shapes=[pltpu.SemaphoreType.DMA((cores, 2))],
        compiler_params=PARAMS,
    )(*pinned)


def stack_kernel(*refs):
    parts, out_ref, sems = refs[:-2], refs[-2], refs[-1]
    rows = parts[0].shape[0]
    run_copies(
        [
            pltpu.make_async_copy(part, out_ref.at[at * rows : (at + 1) * rows], sems.at[at])
            for at, part in enumerate(parts)
        ]
    )


def stack(parts):
    rows, columns = parts[0].shape
    return pl.pallas_call(
        stack_kernel,
        in_specs=[IN_VMEM] * len(parts),
        out_specs=IN_VMEM,
        out_shape=jax.ShapeDtypeStruct((len(parts) * rows, columns), parts[0].dtype),
        scratch_shapes=[pltpu.SemaphoreType.DMA((len(parts),))],
        compiler_params=PARAMS,
    )(*parts)


def join_kernel(cores, *refs):
    parts, out_ref, sems = refs[1:-2], refs[-2], refs[-1]
    columns = parts[0].shape[1]
    core = lax.axis_index("ulysses")
    copies = []
    for at, part in enumerate(parts):
        place = pl.multiple_of(lax.rem(core + cores - at - 1, cores) * columns, columns)
        copies.append(pltpu.make_async_copy(part, out_ref.at[:, pl.ds(place, columns)], sems.at[at]))
    run_copies(copies)


def join(cores, out, parts):
    return pl.pallas_call(
        functools.partial(join_kernel, cores),
        in_specs=[ANYWHERE] + [IN_VMEM] * len(parts),
        out_specs=ANYWHERE,
        out_shape=jax.ShapeDtypeStruct(out.shape, out.dtype),
        scratch_shapes=[pltpu.SemaphoreType.DMA((len(parts),))],
        input_output_aliases={0: 0},
        compiler_params=PARAMS,
    )(out, *parts)


def bits(table_ref, row, low):
    word = jnp.int32(0)
    for index in range(table_ref.shape[1]):
        entry = table_ref[row, index] - low
        inside = (entry >= 0) & (entry < 32)
        word = word | jnp.where(inside, lax.shift_left(jnp.int32(1), jnp.where(inside, entry, 0)), 0)
    return word


def bit_at(word, place):
    return lax.shift_right_logical(word, place) & 1


def chunk_kernel(sizes, units, first, last, turns, *refs):
    cores, pair, groups, per_group, block, blocks = sizes
    table_hbm, scale_hbm, *query_hbm = refs[: 2 + cores]
    unit_refs = refs[2 + cores : 2 + cores + len(units)]
    rest = refs[2 + cores + len(units) :]
    old = None
    if not first:
        old, rest = rest[:3], rest[3:]
    if last:
        out_hbm, rest = rest[: len(turns)], rest[len(turns) :]
    else:
        new, rest = rest[:3], rest[3:]
    query_ref, tile_ref, values_ref, slot_ref, count_ref, mask_ref, table_ref, scale_ref, sems, table_sems = rest[:10]
    if last:
        out_ref, out_sems = rest[10:]
    groups_here = groups // cores
    width = per_group * block
    wide = per_group * DH
    words = -(-blocks // 32)
    slots = len(units) * cores
    core = lax.axis_index("ulysses")
    span = lax.axis_index("blk")
    line, side = lax.div(span, pair), lax.rem(span, pair)
    spans = []
    for back, other in units:
        at_line = line - back
        spans.append(jnp.where(at_line >= 0, at_line * pair + (pair - 1 - side if other else side), -1))
    steps = len(turns) * groups_here

    def turn_at(step):
        return turns[0] - lax.div(step, groups_here), lax.rem(step, groups_here)

    def row_of(turn):
        return lax.rem(core + turn, cores)

    def by_turn(step, act):
        turn, group = turn_at(step)
        for index, at in enumerate(turns):

            @pl.when(turn == at)
            def _(index=index, at=at):
                act(index, at, group)

    def query_copy(at, group, buffer):
        place = (core * groups_here + group) * wide
        source = query_hbm[at].at[:, pl.ds(pl.multiple_of(place, wide), wide)]
        return pltpu.make_async_copy(source, query_ref.at[buffer], sems.at[0, buffer])

    def out_copy(index, at, group, buffer):
        place = (core * groups_here + group if at == 0 else group) * wide
        target = out_hbm[index].at[:, pl.ds(pl.multiple_of(place, wide), wide)]
        return pltpu.make_async_copy(out_ref.at[buffer], target, out_sems.at[buffer])

    def tile_copy(unit, part, group, buffer, at):
        column = pl.ds(pl.multiple_of(group * DH, DH), DH)
        rows = pl.ds(pl.multiple_of(part * (2 * block), 2 * block), 2 * block)
        return pltpu.make_async_copy(unit_refs[unit].at[rows, column], tile_ref.at[buffer, at], sems.at[1, buffer])

    by_turn(0, lambda index, at, group: query_copy(at, group, 0).start())
    run_copies(
        [
            pltpu.make_async_copy(table_hbm, table_ref, table_sems.at[0]),
            pltpu.make_async_copy(scale_hbm, scale_ref, table_sems.at[1]),
        ]
    )

    for group in range(groups_here):
        mask_ref[group, 0] = bits(table_ref, groups + core * groups_here + group, 0)
        for word in range(words):
            mask_ref[group, 1 + word] = bits(table_ref, core * groups_here + group, word * 32)

    def fetch(step, buffer):
        turn, group = turn_at(step)
        here = span * cores + row_of(turn)
        slash_bits = mask_ref[group, 0]
        count = jnp.int32(0)
        for unit in range(len(units)):
            for ahead in range(cores):
                part = lax.rem(turn + ahead, cores)
                place = spans[unit] * cores + lax.rem(core + part, cores)
                back = here - place
                valid = (spans[unit] >= 0) & (back >= 0)
                at = jnp.where(valid, place, 0)
                vertical_bits = mask_ref[group, 1 + lax.shift_right_logical(at, 5)]
                near = jnp.where(back < 32, bit_at(slash_bits, back & 31), 0)
                live = jnp.where(valid, near | bit_at(vertical_bits, at & 31), 0)

                @pl.when(live > 0)
                def _(unit=unit, part=part, count=count, place=place):
                    tile_copy(unit, part, group, buffer, count).start()
                    slot_ref[buffer, count] = place

                count = count + live
        count_ref[buffer] = count

    fetch(0, 0)

    @pl.loop(0, steps)
    def _(step):
        buffer = lax.rem(step, 2)

        @pl.when(step + 1 < steps)
        def _():
            by_turn(step + 1, lambda index, at, group: query_copy(at, group, 1 - buffer).start())
            fetch(step + 1, 1 - buffer)

        turn, group = turn_at(step)
        query_copy(turns[0], 0, buffer).wait()
        count = count_ref[buffer]
        for at in range(slots):

            @pl.when(at < count)
            def _(at=at):
                tile_copy(0, 0, 0, buffer, at).wait()

        own_group = core * groups_here + group
        head_base = own_group * per_group
        scale_row = row_of(turn)

        def scale_at(slot, head):
            return scale_ref[scale_row, head_base + head] * scale_ref[cores + slot_ref[buffer, slot], own_group] * LOG2E

        if last:

            @pl.when(step >= 2)
            def _():
                out_copy(0, turns[0], 0, buffer).wait()

        def finish(head, total_values, total):
            done = total_values * (1.0 / total)
            out_ref[buffer, :, head * DH : (head + 1) * DH] = done.T.astype(BF16)

        base = pl.multiple_of((turn * groups_here + group) * width, width)
        for many in range(1, slots + 1):

            @pl.when(count == many)
            def _(many=many):
                for at in range(many):
                    values_ref[:, at * block : (at + 1) * block] = tile_ref[buffer, at, block : 2 * block, :].T
                attend(
                    many,
                    first,
                    block,
                    per_group,
                    scale_at,
                    jnp.concatenate([tile_ref[buffer, at, 0:block, :] for at in range(many)], axis=0),
                    values_ref[:, 0 : many * block],
                    query_ref.at[buffer],
                    None if first else (old, base),
                    None if last else (new, base),
                    finish if last else None,
                )

        if last:
            if not first:

                @pl.when(count == 0)
                def _():
                    for head in range(per_group):
                        at = pl.ds(base + head * block, block)
                        finish(head, old[2][:, at], old[1][:, at])

            by_turn(step, lambda index, at, group: out_copy(index, at, group, buffer).start())

    if last:
        for step in range(max(0, steps - 2), steps):
            out_copy(0, turns[0], 0, step % 2).wait()


def attend_chunk(sizes, table, scales, queries, units, arrays, state, turns, last):
    cores, pair, groups, per_group, block, blocks = sizes
    first = state is None
    width = per_group * block
    slots = len(units) * cores
    kernel = functools.partial(chunk_kernel, sizes, units, first, last, turns)
    places = cores * (groups // cores)
    state_shape = [
        jax.ShapeDtypeStruct((1, places * width), F32),
        jax.ShapeDtypeStruct((1, places * width), F32),
        jax.ShapeDtypeStruct((DH, places * width), F32),
    ]
    own, others = queries[0].shape, (block, queries[0].shape[1] // cores)
    out_shape = [jax.ShapeDtypeStruct(own if turn == 0 else others, BF16) for turn in turns]
    scratch = [
        pltpu.VMEM((2, block, per_group * DH), BF16),
        pltpu.VMEM((2, slots, 2 * block, DH), BF16),
        pltpu.VMEM((DH, slots * block), BF16),
        pltpu.SMEM((2, slots), jnp.int32),
        pltpu.SMEM((2,), jnp.int32),
        pltpu.SMEM((groups // cores, 1 + -(-blocks // 32)), jnp.int32),
        pltpu.SMEM(table.shape, jnp.int32),
        pltpu.SMEM(scales.shape, F32),
        pltpu.SemaphoreType.DMA((2, 2)),
        pltpu.SemaphoreType.DMA((2,)),
    ]
    if last:
        scratch += [
            pltpu.VMEM((2, block, per_group * DH), BF16),
            pltpu.SemaphoreType.DMA((2,)),
        ]
    base = 2 + cores + len(units)
    return pl.pallas_call(
        kernel,
        in_specs=[ANYWHERE] * (2 + cores + len(units)) + ([] if first else [IN_VMEM] * 3),
        out_specs=[ANYWHERE] * len(turns) if last else [IN_VMEM] * 3,
        out_shape=out_shape if last else state_shape,
        scratch_shapes=scratch,
        input_output_aliases={} if first or last else {base + i: i for i in range(3)},
        compiler_params=PARAMS,
        cost_estimate=pl.CostEstimate(flops=1, bytes_accessed=0, transcendentals=0),
    )(table, scales, *queries, *arrays, *(() if first else state))


def local(spans, cores, query_int, key_int, values, query_scale, key_scale, verticals, slashes):
    block = query_int.shape[0]
    groups, blocks = verticals.shape[0], key_scale.shape[0]
    per_group = query_int.shape[1] // DH // groups
    columns = query_int.shape[1] // cores
    pair = 2 if spans % 2 == 0 else 1
    lines = spans // pair
    core = lax.axis_index("ulysses")
    sizes = (cores, pair, groups, per_group, block, blocks)

    turned = [[(c, (c - step) % cores) for c in range(cores)] for step in range(cores)]
    back = [[(c, (c + step) % cores) for c in range(cores)] for step in range(cores)]
    shares = deal(cores, key_int, values)
    own = stack(
        [shares[0]] + [lax.ppermute(shares[step], "ulysses", turned[step]) for step in range(1, cores)]
    )
    waiting, _ = lax.optimization_barrier((query_int, own))
    queries = [query_int] + [lax.ppermute(waiting, "ulysses", turned[step]) for step in range(1, cores)]
    table = jnp.concatenate([verticals, slashes], axis=0)
    key_scales = jnp.pad(key_scale, ((0, 0), (0, query_scale.shape[1] - groups)))
    scales = jnp.concatenate([query_scale, key_scales], axis=0).astype(F32)

    climb = [(s, s + pair) for s in range(spans - pair)]
    swap = [(s, s ^ 1) for s in range(spans)]
    turns = tuple(range(cores - 1, -1, -1))
    climbed, crossed, state = own, None, None
    steps = lines + (pair == 2)
    for step in range(steps):
        last = step + 1 == steps
        sent, arrived = climbed, crossed
        climbed = lax.ppermute(sent, "blk", climb) if step + 1 < lines else None
        crossed = lax.ppermute(sent, "blk", swap) if pair == 2 and sent is not None else None
        units, arrays = [], []
        if sent is not None:
            units.append((step, False))
            arrays.append(sent)
        if arrived is not None:
            units.append((step - 1, True))
            arrays.append(arrived)
        run = functools.partial(attend_chunk, sizes, table, scales, queries, tuple(units), arrays, state)
        if not last:
            state = run(turns, False)
            climbed, crossed, state = lax.optimization_barrier((climbed, crossed, state))
    if cores == 1:
        return run(turns, True)[0]
    others = run(turns[:-1], True)
    out = run(turns[-1:], True)[0]
    arrived = [
        lax.ppermute(one, "ulysses", back[turn]) for turn, one in sorted(zip(turns[:-1], others), key=lambda x: x[0])
    ]
    return join(cores, out, arrived)


def solution(mesh):
    rows = P(("group", "blk", "ulysses"), None)
    in_specs = (rows, rows, rows, P(("group", "blk"), None), P("group", None), P("group", None), P("group", None))
    run = functools.partial(local, mesh.shape["blk"], mesh.shape["ulysses"])
    return jax.shard_map(run, mesh=mesh, in_specs=in_specs, out_specs=rows, check_vma=False)
```

```python
import functools

import jax
import jax.numpy as jnp
from jax import lax
from jax.experimental import pallas as pl
from jax.experimental.pallas import tpu as pltpu
from jax.sharding import PartitionSpec as P

DH = 128
FLOOR_SCORE = -1e30
LOG2E = 1.4426950408889634
NT = (((1,), (1,)), ((), ()))
F32 = jnp.float32
BF16 = jnp.bfloat16
VMEM_LIMIT = 16 * 2**20
ANYWHERE = pl.BlockSpec(memory_space=pl.ANY)
IN_VMEM = pl.BlockSpec(memory_space=pltpu.VMEM)
PARAMS = pltpu.CompilerParams(vmem_limit_bytes=VMEM_LIMIT)


def along_rows(combine, parts):
    rows = [part[at : at + 8] for part in parts for at in range(0, part.shape[0], 8)]
    lanes = rows[:4]
    for at, row in enumerate(rows[4:]):
        lanes[at % 4] = combine(lanes[at % 4], row)
    return functools.reduce(combine, lanes)


def attend(count, diagonal, block, per_group, scale_at, keys, values, query_ref, before, after, finish):
    abreast = 2 if count == 1 and per_group % 2 == 0 else 1

    def dots_of(head):
        queries = [query_ref[:, at * DH : (at + 1) * DH] for at in range(head, head + abreast)]
        return lax.dot_general(keys, jnp.concatenate(queries, axis=0), NT, preferred_element_type=F32)

    def weigh(head, dots):
        probs, shrinks, totals = [], [], []
        for at in range(abreast):
            parts = []
            for slot in range(count):
                part = dots[slot * block : (slot + 1) * block, at * block : (at + 1) * block]
                part = part * scale_at(slot, head + at)
                if diagonal and slot == 0:
                    key_at = lax.broadcasted_iota(jnp.int32, part.shape, 0)
                    query_at = lax.broadcasted_iota(jnp.int32, part.shape, 1)
                    part = jnp.where(key_at <= query_at, part, FLOOR_SCORE)
                parts.append(part)
            most = jnp.max(along_rows(jnp.maximum, parts), axis=0, keepdims=True)
            if before is not None:
                there = pl.ds(before[1] + (head + at) * block, block)
                old = before[0][0][:, there]
                most = jnp.maximum(most, old)
                shrinks.append(jnp.exp2(old - most))
            weights = [jnp.exp2(part - most) for part in parts]
            total = jnp.sum(along_rows(jnp.add, weights), axis=0, keepdims=True)
            if before is not None:
                total = total + before[0][1][:, there] * shrinks[-1]
            if after is not None:
                here = pl.ds(after[1] + (head + at) * block, block)
                after[0][0][:, here] = most
                after[0][1][:, here] = total
            totals.append(total)
            probs.append(jnp.concatenate([part.astype(BF16) for part in weights], axis=0))
        shrink = None if before is None else jnp.concatenate(shrinks, axis=1)
        return jnp.concatenate(probs, axis=1), shrink, jnp.concatenate(totals, axis=1)

    def gather(head, probs, shrink, total):
        add = jnp.dot(values, probs, preferred_element_type=F32)
        if before is not None:
            add = before[0][2][:, pl.ds(before[1] + head * block, abreast * block)] * shrink + add
        if finish is None:
            after[0][2][:, pl.ds(after[1] + head * block, abreast * block)] = add
            return
        for at in range(abreast):
            part = slice(at * block, (at + 1) * block)
            finish(head + at, add[:, part], total[:, part])

    dots = dots_of(0)
    pending = None
    for head in range(0, per_group, abreast):
        ahead = dots_of(head + abreast) if head + abreast < per_group else None
        if pending is not None:
            gather(*pending)
        pending = (head,) + weigh(head, dots)
        dots = ahead
    gather(*pending)


def run_copies(copies):
    for copy in copies:
        copy.start()
    for copy in copies:
        copy.wait()


def deal_kernel(cores, key_ref, value_ref, *rest):
    shares, sems = rest[:-1], rest[-1]
    rows, columns = key_ref.shape[0], key_ref.shape[1] // cores
    core = lax.axis_index("ulysses")
    copies = []
    for step, share in enumerate(shares):
        part = pl.ds(pl.multiple_of(lax.rem(core + cores - step, cores) * columns, columns), columns)
        copies.append(pltpu.make_async_copy(key_ref.at[:, part], share.at[0:rows], sems.at[step, 0]))
        copies.append(pltpu.make_async_copy(value_ref.at[:, part], share.at[rows : 2 * rows], sems.at[step, 1]))
    run_copies(copies)


def deal(cores, key_int, values):
    rows, columns = key_int.shape
    pinned = [pltpu.with_memory_space_constraint(array, pltpu.HBM) for array in (key_int, values)]
    return pl.pallas_call(
        functools.partial(deal_kernel, cores),
        in_specs=[ANYWHERE] * 2,
        out_specs=[IN_VMEM] * cores,
        out_shape=[jax.ShapeDtypeStruct((2 * rows, columns // cores), key_int.dtype)] * cores,
        scratch_shapes=[pltpu.SemaphoreType.DMA((cores, 2))],
        compiler_params=PARAMS,
    )(*pinned)


def stack_kernel(*refs):
    parts, out_ref, sems = refs[:-2], refs[-2], refs[-1]
    rows = parts[0].shape[0]
    run_copies(
        [
            pltpu.make_async_copy(part, out_ref.at[at * rows : (at + 1) * rows], sems.at[at])
            for at, part in enumerate(parts)
        ]
    )


def stack(parts):
    rows, columns = parts[0].shape
    return pl.pallas_call(
        stack_kernel,
        in_specs=[IN_VMEM] * len(parts),
        out_specs=IN_VMEM,
        out_shape=jax.ShapeDtypeStruct((len(parts) * rows, columns), parts[0].dtype),
        scratch_shapes=[pltpu.SemaphoreType.DMA((len(parts),))],
        compiler_params=PARAMS,
    )(*parts)


def join_kernel(cores, *refs):
    parts, out_ref, sems = refs[1:-2], refs[-2], refs[-1]
    columns = parts[0].shape[1]
    core = lax.axis_index("ulysses")
    copies = []
    for at, part in enumerate(parts):
        place = pl.multiple_of(lax.rem(core + cores - at - 1, cores) * columns, columns)
        copies.append(pltpu.make_async_copy(part, out_ref.at[:, pl.ds(place, columns)], sems.at[at]))
    run_copies(copies)


def join(cores, out, parts):
    return pl.pallas_call(
        functools.partial(join_kernel, cores),
        in_specs=[ANYWHERE] + [IN_VMEM] * len(parts),
        out_specs=ANYWHERE,
        out_shape=jax.ShapeDtypeStruct(out.shape, out.dtype),
        scratch_shapes=[pltpu.SemaphoreType.DMA((len(parts),))],
        input_output_aliases={0: 0},
        compiler_params=PARAMS,
    )(out, *parts)


def bits(rows, low):
    entries = rows - low
    inside = (entries >= 0) & (entries < 32)
    return jnp.sum(jnp.where(inside, lax.shift_left(jnp.ones_like(entries), entries & 31), 0), axis=1)


def bit_at(word, place):
    return lax.shift_right_logical(word, place) & 1


def chunk_kernel(sizes, units, first, last, turns, *refs):
    cores, pair, groups, per_group, block = sizes
    table_hbm, scale_hbm, *query_hbm = refs[: 2 + cores]
    unit_refs = refs[2 + cores : 2 + cores + len(units)]
    rest = refs[2 + cores + len(units) :]
    old = None
    if not first:
        old, rest = rest[:3], rest[3:]
    if last:
        out_hbm, rest = rest[: len(turns)], rest[len(turns) :]
    else:
        new, rest = rest[:3], rest[3:]
    query_ref, tile_ref, values_ref, slot_ref, count_ref, table_ref, scale_ref, sems, table_sems = rest[:9]
    if last:
        out_ref, out_sems = rest[9:]
    groups_here = groups // cores
    width = per_group * block
    wide = per_group * DH
    slots = len(units) * cores
    core = lax.axis_index("ulysses")
    span = lax.axis_index("blk")
    line, side = lax.div(span, pair), lax.rem(span, pair)
    spans = []
    for back, other in units:
        at_line = line - back
        spans.append(jnp.where(at_line >= 0, at_line * pair + (pair - 1 - side if other else side), -1))
    steps = len(turns) * groups_here

    def turn_at(step):
        return turns[0] - lax.div(step, groups_here), lax.rem(step, groups_here)

    def row_of(turn):
        return lax.rem(core + turn, cores)

    def by_turn(step, act):
        turn, group = turn_at(step)
        for index, at in enumerate(turns):

            @pl.when(turn == at)
            def _(index=index, at=at):
                act(index, at, group)

    def query_copy(at, group, buffer):
        place = (core * groups_here + group) * wide
        source = query_hbm[at].at[:, pl.ds(pl.multiple_of(place, wide), wide)]
        return pltpu.make_async_copy(source, query_ref.at[buffer], sems.at[0, buffer])

    def out_copy(index, at, group, buffer):
        place = (core * groups_here + group if at == 0 else group) * wide
        target = out_hbm[index].at[:, pl.ds(pl.multiple_of(place, wide), wide)]
        return pltpu.make_async_copy(out_ref.at[buffer], target, out_sems.at[buffer])

    def tile_copy(unit, part, group, buffer, at):
        column = pl.ds(pl.multiple_of(group * DH, DH), DH)
        rows = pl.ds(pl.multiple_of(part * (2 * block), 2 * block), 2 * block)
        return pltpu.make_async_copy(unit_refs[unit].at[rows, column], tile_ref.at[buffer, at], sems.at[1, buffer])

    by_turn(0, lambda index, at, group: query_copy(at, group, 0).start())
    run_copies(
        [
            pltpu.make_async_copy(table_hbm, table_ref, table_sems.at[0]),
            pltpu.make_async_copy(scale_hbm, scale_ref, table_sems.at[1]),
        ]
    )

    def fetch(step, buffer):
        turn, group = turn_at(step)
        here = span * cores + row_of(turn)
        own_group = core * groups_here + group
        slash_bits = table_ref[own_group, 0]
        count = jnp.int32(0)
        for unit in range(len(units)):
            for ahead in range(cores):
                part = lax.rem(turn + ahead, cores)
                place = spans[unit] * cores + lax.rem(core + part, cores)
                back = here - place
                valid = (spans[unit] >= 0) & (back >= 0)
                at = jnp.where(valid, place, 0)
                vertical_bits = table_ref[own_group, 1 + lax.shift_right_logical(at, 5)]
                near = jnp.where(back < 32, bit_at(slash_bits, back & 31), 0)
                live = jnp.where(valid, near | bit_at(vertical_bits, at & 31), 0)

                @pl.when(live > 0)
                def _(unit=unit, part=part, count=count, place=place):
                    tile_copy(unit, part, group, buffer, count).start()
                    slot_ref[buffer, count] = place

                count = count + live
        count_ref[buffer] = count

    fetch(0, 0)

    @pl.loop(0, steps)
    def _(step):
        buffer = lax.rem(step, 2)

        @pl.when(step + 1 < steps)
        def _():
            by_turn(step + 1, lambda index, at, group: query_copy(at, group, 1 - buffer).start())
            fetch(step + 1, 1 - buffer)

        turn, group = turn_at(step)
        query_copy(turns[0], 0, buffer).wait()
        count = count_ref[buffer]
        for at in range(slots):

            @pl.when(at < count)
            def _(at=at):
                tile_copy(0, 0, 0, buffer, at).wait()

        own_group = core * groups_here + group
        head_base = own_group * per_group
        scale_row = row_of(turn)

        def scale_at(slot, head):
            return scale_ref[scale_row, head_base + head] * scale_ref[cores + slot_ref[buffer, slot], own_group] * LOG2E

        if last:

            @pl.when(step >= 2)
            def _():
                out_copy(0, turns[0], 0, buffer).wait()

        def finish(head, total_values, total):
            done = total_values * (1.0 / total)
            out_ref[buffer, :, head * DH : (head + 1) * DH] = done.T.astype(BF16)

        base = pl.multiple_of((turn * groups_here + group) * width, width)
        for many in range(1, slots + 1):

            @pl.when(count == many)
            def _(many=many):
                for at in range(many):
                    values_ref[:, at * block : (at + 1) * block] = tile_ref[buffer, at, block : 2 * block, :].T
                attend(
                    many,
                    first,
                    block,
                    per_group,
                    scale_at,
                    jnp.concatenate([tile_ref[buffer, at, 0:block, :] for at in range(many)], axis=0),
                    values_ref[:, 0 : many * block],
                    query_ref.at[buffer],
                    None if first else (old, base),
                    None if last else (new, base),
                    finish if last else None,
                )

        if last:
            if not first:

                @pl.when(count == 0)
                def _():
                    for head in range(per_group):
                        at = pl.ds(base + head * block, block)
                        finish(head, old[2][:, at], old[1][:, at])

            by_turn(step, lambda index, at, group: out_copy(index, at, group, buffer).start())

    if last:
        for step in range(max(0, steps - 2), steps):
            out_copy(0, turns[0], 0, step % 2).wait()


def attend_chunk(sizes, table, scales, queries, units, arrays, state, turns, last):
    cores, pair, groups, per_group, block = sizes
    first = state is None
    width = per_group * block
    slots = len(units) * cores
    kernel = functools.partial(chunk_kernel, sizes, units, first, last, turns)
    places = cores * (groups // cores)
    state_shape = [
        jax.ShapeDtypeStruct((1, places * width), F32),
        jax.ShapeDtypeStruct((1, places * width), F32),
        jax.ShapeDtypeStruct((DH, places * width), F32),
    ]
    own, others = queries[0].shape, (block, queries[0].shape[1] // cores)
    out_shape = [jax.ShapeDtypeStruct(own if turn == 0 else others, BF16) for turn in turns]
    scratch = [
        pltpu.VMEM((2, block, per_group * DH), BF16),
        pltpu.VMEM((2, slots, 2 * block, DH), BF16),
        pltpu.VMEM((DH, slots * block), BF16),
        pltpu.SMEM((2, slots), jnp.int32),
        pltpu.SMEM((2,), jnp.int32),
        pltpu.SMEM(table.shape, jnp.int32),
        pltpu.SMEM(scales.shape, F32),
        pltpu.SemaphoreType.DMA((2, 2)),
        pltpu.SemaphoreType.DMA((2,)),
    ]
    if last:
        scratch += [
            pltpu.VMEM((2, block, per_group * DH), BF16),
            pltpu.SemaphoreType.DMA((2,)),
        ]
    base = 2 + cores + len(units)
    return pl.pallas_call(
        kernel,
        in_specs=[ANYWHERE] * (2 + cores + len(units)) + ([] if first else [IN_VMEM] * 3),
        out_specs=[ANYWHERE] * len(turns) if last else [IN_VMEM] * 3,
        out_shape=out_shape if last else state_shape,
        scratch_shapes=scratch,
        input_output_aliases={} if first or last else {base + i: i for i in range(3)},
        compiler_params=PARAMS,
        cost_estimate=pl.CostEstimate(flops=1, bytes_accessed=0, transcendentals=0),
    )(table, scales, *queries, *arrays, *(() if first else state))


def local(spans, cores, query_int, key_int, values, query_scale, key_scale, verticals, slashes):
    block = query_int.shape[0]
    groups, blocks = verticals.shape[0], key_scale.shape[0]
    per_group = query_int.shape[1] // DH // groups
    columns = query_int.shape[1] // cores
    pair = 2 if spans % 2 == 0 else 1
    lines = spans // pair
    core = lax.axis_index("ulysses")
    sizes = (cores, pair, groups, per_group, block)

    turned = [[(c, (c - step) % cores) for c in range(cores)] for step in range(cores)]
    back = [[(c, (c + step) % cores) for c in range(cores)] for step in range(cores)]
    shares = deal(cores, key_int, values)
    own = stack(
        [shares[0]] + [lax.ppermute(shares[step], "ulysses", turned[step]) for step in range(1, cores)]
    )
    waiting, _ = lax.optimization_barrier((query_int, own))
    queries = [query_int] + [lax.ppermute(waiting, "ulysses", turned[step]) for step in range(1, cores)]
    words = [bits(slashes, 0)] + [bits(verticals, low) for low in range(0, blocks, 32)]
    table = jnp.stack(words, axis=1).astype(jnp.int32)
    key_scales = jnp.pad(key_scale, ((0, 0), (0, query_scale.shape[1] - groups)))
    scales = jnp.concatenate([query_scale, key_scales], axis=0).astype(F32)

    climb = [(s, (s + pair) % spans) for s in range(spans)]
    swap = [(s, s ^ 1) for s in range(spans)]
    turns = tuple(range(cores - 1, -1, -1))
    climbed, crossed, state = own, None, None
    steps = lines + (pair == 2)
    for step in range(steps):
        last = step + 1 == steps
        sent, arrived = climbed, crossed
        climbed = lax.ppermute(sent, "blk", climb) if step + 1 < lines else None
        crossed = lax.ppermute(sent, "blk", swap) if pair == 2 and sent is not None else None
        units, arrays = [], []
        if sent is not None:
            units.append((step, False))
            arrays.append(sent)
        if arrived is not None:
            units.append((step - 1, True))
            arrays.append(arrived)
        run = functools.partial(attend_chunk, sizes, table, scales, queries, tuple(units), arrays, state)
        if not last:
            state = run(turns, False)
            state, crossed, climbed = lax.optimization_barrier((state, crossed, climbed))
    if cores == 1:
        return run(turns, True)[0]
    others = run(turns[:-1], True)
    out = run(turns[-1:], True)[0]
    arrived = [
        lax.ppermute(one, "ulysses", back[turn]) for turn, one in sorted(zip(turns[:-1], others), key=lambda x: x[0])
    ]
    return join(cores, out, arrived)


def solution(mesh):
    rows = P(("group", "blk", "ulysses"), None)
    in_specs = (rows, rows, rows, P(("group", "blk"), None), P("group", None), P("group", None), P("group", None))
    run = functools.partial(local, mesh.shape["blk"], mesh.shape["ulysses"])
    return jax.shard_map(run, mesh=mesh, in_specs=in_specs, out_specs=rows, check_vma=False)
```

```python
import functools

import jax
import jax.numpy as jnp
from jax import lax
from jax.experimental import pallas as pl
from jax.experimental.pallas import tpu as pltpu
from jax.sharding import PartitionSpec as P

DH = 128
FLOOR_SCORE = -1e30
LOG2E = 1.4426950408889634
NT = (((1,), (1,)), ((), ()))
F32 = jnp.float32
BF16 = jnp.bfloat16
VMEM_LIMIT = 16 * 2**20
ANYWHERE = pl.BlockSpec(memory_space=pl.ANY)
IN_VMEM = pl.BlockSpec(memory_space=pltpu.VMEM)
PARAMS = pltpu.CompilerParams(vmem_limit_bytes=VMEM_LIMIT)


def along_rows(combine, parts):
    rows = [part[at : at + 8] for part in parts for at in range(0, part.shape[0], 8)]
    lanes = rows[:4]
    for at, row in enumerate(rows[4:]):
        lanes[at % 4] = combine(lanes[at % 4], row)
    return functools.reduce(combine, lanes)


def attend(count, diagonal, block, per_group, scale_at, keys, values, query_ref, before, after, finish):
    abreast = 2 if count == 1 and per_group % 2 == 0 else 1

    def dots_of(head):
        queries = [query_ref[:, at * DH : (at + 1) * DH] for at in range(head, head + abreast)]
        return lax.dot_general(keys, jnp.concatenate(queries, axis=0), NT, preferred_element_type=F32)

    def weigh(head, dots):
        probs, shrinks, totals = [], [], []
        for at in range(abreast):
            parts = []
            for slot in range(count):
                part = dots[slot * block : (slot + 1) * block, at * block : (at + 1) * block]
                part = part * scale_at(slot, head + at)
                if diagonal and slot == 0:
                    key_at = lax.broadcasted_iota(jnp.int32, part.shape, 0)
                    query_at = lax.broadcasted_iota(jnp.int32, part.shape, 1)
                    part = jnp.where(key_at <= query_at, part, FLOOR_SCORE)
                parts.append(part)
            most = jnp.max(along_rows(jnp.maximum, parts), axis=0, keepdims=True)
            if before is not None:
                there = pl.ds(before[1] + (head + at) * block, block)
                old = before[0][0][:, there]
                most = jnp.maximum(most, old)
                shrinks.append(jnp.exp2(old - most))
            weights = [jnp.exp2(part - most) for part in parts]
            total = jnp.sum(along_rows(jnp.add, weights), axis=0, keepdims=True)
            if before is not None:
                total = total + before[0][1][:, there] * shrinks[-1]
            if after is not None:
                here = pl.ds(after[1] + (head + at) * block, block)
                after[0][0][:, here] = most
                after[0][1][:, here] = total
            totals.append(total)
            probs.append(jnp.concatenate([part.astype(BF16) for part in weights], axis=0))
        shrink = None if before is None else jnp.concatenate(shrinks, axis=1)
        return jnp.concatenate(probs, axis=1), shrink, jnp.concatenate(totals, axis=1)

    def gather(head, probs, shrink, total):
        add = jnp.dot(values, probs, preferred_element_type=F32)
        if before is not None:
            add = before[0][2][:, pl.ds(before[1] + head * block, abreast * block)] * shrink + add
        if finish is None:
            after[0][2][:, pl.ds(after[1] + head * block, abreast * block)] = add
            return
        for at in range(abreast):
            part = slice(at * block, (at + 1) * block)
            finish(head + at, add[:, part], total[:, part])

    dots = dots_of(0)
    pending = None
    for head in range(0, per_group, abreast):
        ahead = dots_of(head + abreast) if head + abreast < per_group else None
        if pending is not None:
            gather(*pending)
        pending = (head,) + weigh(head, dots)
        dots = ahead
    gather(*pending)


def run_copies(copies):
    for copy in copies:
        copy.start()
    for copy in copies:
        copy.wait()


def deal_kernel(cores, key_ref, value_ref, *rest):
    shares, sems = rest[:-1], rest[-1]
    rows, columns = key_ref.shape[0], key_ref.shape[1] // cores
    core = lax.axis_index("ulysses")
    copies = []
    for step, share in enumerate(shares):
        part = pl.ds(pl.multiple_of(lax.rem(core + cores - step, cores) * columns, columns), columns)
        copies.append(pltpu.make_async_copy(key_ref.at[:, part], share.at[0:rows], sems.at[step, 0]))
        copies.append(pltpu.make_async_copy(value_ref.at[:, part], share.at[rows : 2 * rows], sems.at[step, 1]))
    run_copies(copies)


def deal(cores, key_int, values):
    rows, columns = key_int.shape
    pinned = [pltpu.with_memory_space_constraint(array, pltpu.HBM) for array in (key_int, values)]
    return pl.pallas_call(
        functools.partial(deal_kernel, cores),
        in_specs=[ANYWHERE] * 2,
        out_specs=[IN_VMEM] * cores,
        out_shape=[jax.ShapeDtypeStruct((2 * rows, columns // cores), key_int.dtype)] * cores,
        scratch_shapes=[pltpu.SemaphoreType.DMA((cores, 2))],
        compiler_params=PARAMS,
    )(*pinned)


def stack_kernel(*refs):
    parts, out_ref, sems = refs[:-2], refs[-2], refs[-1]
    rows = parts[0].shape[0]
    run_copies(
        [
            pltpu.make_async_copy(part, out_ref.at[at * rows : (at + 1) * rows], sems.at[at])
            for at, part in enumerate(parts)
        ]
    )


def stack(parts):
    rows, columns = parts[0].shape
    return pl.pallas_call(
        stack_kernel,
        in_specs=[IN_VMEM] * len(parts),
        out_specs=IN_VMEM,
        out_shape=jax.ShapeDtypeStruct((len(parts) * rows, columns), parts[0].dtype),
        scratch_shapes=[pltpu.SemaphoreType.DMA((len(parts),))],
        compiler_params=PARAMS,
    )(*parts)


def join_kernel(cores, *refs):
    parts, out_ref, sems = refs[1:-2], refs[-2], refs[-1]
    columns = parts[0].shape[1]
    core = lax.axis_index("ulysses")
    copies = []
    for at, part in enumerate(parts):
        place = pl.multiple_of(lax.rem(core + cores - at - 1, cores) * columns, columns)
        copies.append(pltpu.make_async_copy(part, out_ref.at[:, pl.ds(place, columns)], sems.at[at]))
    run_copies(copies)


def join(cores, out, parts):
    return pl.pallas_call(
        functools.partial(join_kernel, cores),
        in_specs=[ANYWHERE] + [IN_VMEM] * len(parts),
        out_specs=ANYWHERE,
        out_shape=jax.ShapeDtypeStruct(out.shape, out.dtype),
        scratch_shapes=[pltpu.SemaphoreType.DMA((len(parts),))],
        input_output_aliases={0: 0},
        compiler_params=PARAMS,
    )(out, *parts)


def bits(rows, low):
    entries = rows - low
    inside = (entries >= 0) & (entries < 32)
    return jnp.sum(jnp.where(inside, lax.shift_left(jnp.ones_like(entries), entries & 31), 0), axis=1)


def bit_at(word, place):
    return lax.shift_right_logical(word, place) & 1


def chunk_kernel(sizes, units, first, last, turns, *refs):
    cores, pair, groups, per_group, block = sizes
    table_hbm, scale_hbm, *query_hbm = refs[: 2 + cores]
    unit_refs = refs[2 + cores : 2 + cores + len(units)]
    rest = refs[2 + cores + len(units) :]
    old = None
    if not first:
        old, rest = rest[:3], rest[3:]
    if last:
        out_hbm, rest = rest[: len(turns)], rest[len(turns) :]
    else:
        new, rest = rest[:3], rest[3:]
    query_ref, tile_ref, values_ref, slot_ref, place_ref, table_ref, scale_ref, sems, table_sems = rest[:9]
    if last:
        out_ref, out_sems = rest[9:]
    groups_here = groups // cores
    width = per_group * block
    wide = per_group * DH
    slots = len(units) * cores
    core = lax.axis_index("ulysses")
    span = lax.axis_index("blk")
    line, side = lax.div(span, pair), lax.rem(span, pair)
    spans = []
    for back, other in units:
        at_line = line - back
        spans.append(jnp.where(at_line >= 0, at_line * pair + (pair - 1 - side if other else side), -1))
    steps = len(turns) * groups_here

    def turn_at(step):
        return turns[0] - lax.div(step, groups_here), lax.rem(step, groups_here)

    def row_of(turn):
        return lax.rem(core + turn, cores)

    def by_turn(step, act):
        turn, group = turn_at(step)
        for index, at in enumerate(turns):

            @pl.when(turn == at)
            def _(index=index, at=at):
                act(index, at, group)

    def query_copy(at, group, buffer):
        place = (core * groups_here + group) * wide
        source = query_hbm[at].at[:, pl.ds(pl.multiple_of(place, wide), wide)]
        return pltpu.make_async_copy(source, query_ref.at[buffer], sems.at[0, buffer])

    def out_copy(index, at, group, buffer):
        place = (core * groups_here + group if at == 0 else group) * wide
        target = out_hbm[index].at[:, pl.ds(pl.multiple_of(place, wide), wide)]
        return pltpu.make_async_copy(out_ref.at[buffer], target, out_sems.at[buffer])

    def part_of(turn, slot):
        return lax.rem(turn + slot, cores) if first else slot % cores

    def tile_copy(slot, part, group, buffer):
        column = pl.ds(pl.multiple_of(group * DH, DH), DH)
        rows = pl.ds(pl.multiple_of(part * (2 * block), 2 * block), 2 * block)
        source = unit_refs[slot // cores].at[rows, column]
        return pltpu.make_async_copy(source, tile_ref.at[buffer, slot], sems.at[1, buffer])

    def fetch(step, buffer):
        by_turn(step, lambda index, at, group: query_copy(at, group, buffer).start())
        turn, group = turn_at(step)
        for slot in range(slots):
            tile_copy(slot, part_of(turn, slot), group, buffer).start()

    def list_live(turn, own_group):
        here = span * cores + row_of(turn)
        slash_bits = table_ref[own_group, 0]
        count = jnp.int32(0)
        for slot in range(slots):
            at_span = spans[slot // cores]
            place = at_span * cores + lax.rem(core + part_of(turn, slot), cores)
            back = here - place
            valid = (at_span >= 0) & (back >= 0)
            at = jnp.where(valid, place, 0)
            near = jnp.where(back < 32, bit_at(slash_bits, back & 31), 0)
            far = bit_at(table_ref[own_group, 1 + lax.shift_right_logical(at, 5)], at & 31)
            slot_ref[count] = slot
            place_ref[count] = at
            count = count + jnp.where(valid, near | far, 0)
        return count

    fetch(0, 0)
    run_copies(
        [
            pltpu.make_async_copy(table_hbm, table_ref, table_sems.at[0]),
            pltpu.make_async_copy(scale_hbm, scale_ref, table_sems.at[1]),
        ]
    )

    @pl.loop(0, steps)
    def _(step):
        buffer = lax.rem(step, 2)

        @pl.when(step + 1 < steps)
        def _():
            fetch(step + 1, 1 - buffer)

        turn, group = turn_at(step)
        count = list_live(turn, core * groups_here + group)
        query_copy(turns[0], 0, buffer).wait()
        for slot in range(slots):
            tile_copy(slot, 0, 0, buffer).wait()

        own_group = core * groups_here + group
        head_base = own_group * per_group
        scale_row = row_of(turn)

        def scale_at(slot, head):
            return scale_ref[scale_row, head_base + head] * scale_ref[cores + place_ref[slot], own_group] * LOG2E

        if last:

            @pl.when(step >= 2)
            def _():
                out_copy(0, turns[0], 0, buffer).wait()

        def finish(head, total_values, total):
            done = total_values * (1.0 / total)
            out_ref[buffer, :, head * DH : (head + 1) * DH] = done.T.astype(BF16)

        base = pl.multiple_of((turn * groups_here + group) * width, width)
        for many in range(1, slots + 1):

            @pl.when(count == many)
            def _(many=many):
                tiles = [slot_ref[at] for at in range(many)]
                for at, tile in enumerate(tiles):
                    values_ref[:, at * block : (at + 1) * block] = tile_ref[buffer, tile, block : 2 * block, :].T
                attend(
                    many,
                    first,
                    block,
                    per_group,
                    scale_at,
                    jnp.concatenate([tile_ref[buffer, tile, 0:block, :] for tile in tiles], axis=0),
                    values_ref[:, 0 : many * block],
                    query_ref.at[buffer],
                    None if first else (old, base),
                    None if last else (new, base),
                    finish if last else None,
                )

        if last:
            if not first:

                @pl.when(count == 0)
                def _():
                    for head in range(per_group):
                        at = pl.ds(base + head * block, block)
                        finish(head, old[2][:, at], old[1][:, at])

            by_turn(step, lambda index, at, group: out_copy(index, at, group, buffer).start())

    if last:
        for step in range(max(0, steps - 2), steps):
            out_copy(0, turns[0], 0, step % 2).wait()


def attend_chunk(sizes, table, scales, queries, units, arrays, state, turns, last):
    cores, pair, groups, per_group, block = sizes
    first = state is None
    width = per_group * block
    slots = len(units) * cores
    kernel = functools.partial(chunk_kernel, sizes, units, first, last, turns)
    places = cores * (groups // cores)
    state_shape = [
        jax.ShapeDtypeStruct((1, places * width), F32),
        jax.ShapeDtypeStruct((1, places * width), F32),
        jax.ShapeDtypeStruct((DH, places * width), F32),
    ]
    own, others = queries[0].shape, (block, queries[0].shape[1] // cores)
    out_shape = [jax.ShapeDtypeStruct(own if turn == 0 else others, BF16) for turn in turns]
    scratch = [
        pltpu.VMEM((2, block, per_group * DH), BF16),
        pltpu.VMEM((2, slots, 2 * block, DH), BF16),
        pltpu.VMEM((DH, slots * block), BF16),
        pltpu.SMEM((slots,), jnp.int32),
        pltpu.SMEM((slots,), jnp.int32),
        pltpu.SMEM(table.shape, jnp.int32),
        pltpu.SMEM(scales.shape, F32),
        pltpu.SemaphoreType.DMA((2, 2)),
        pltpu.SemaphoreType.DMA((2,)),
    ]
    if last:
        scratch += [
            pltpu.VMEM((2, block, per_group * DH), BF16),
            pltpu.SemaphoreType.DMA((2,)),
        ]
    base = 2 + cores + len(units)
    return pl.pallas_call(
        kernel,
        in_specs=[ANYWHERE] * (2 + cores + len(units)) + ([] if first else [IN_VMEM] * 3),
        out_specs=[ANYWHERE] * len(turns) if last else [IN_VMEM] * 3,
        out_shape=out_shape if last else state_shape,
        scratch_shapes=scratch,
        input_output_aliases={} if first or last else {base + i: i for i in range(3)},
        compiler_params=PARAMS,
        cost_estimate=pl.CostEstimate(flops=1, bytes_accessed=0, transcendentals=0),
    )(table, scales, *queries, *arrays, *(() if first else state))


def local(spans, cores, query_int, key_int, values, query_scale, key_scale, verticals, slashes):
    block = query_int.shape[0]
    groups, blocks = verticals.shape[0], key_scale.shape[0]
    per_group = query_int.shape[1] // DH // groups
    columns = query_int.shape[1] // cores
    pair = 2 if spans % 2 == 0 else 1
    lines = spans // pair
    core = lax.axis_index("ulysses")
    sizes = (cores, pair, groups, per_group, block)

    turned = [[(c, (c - step) % cores) for c in range(cores)] for step in range(cores)]
    back = [[(c, (c + step) % cores) for c in range(cores)] for step in range(cores)]
    shares = deal(cores, key_int, values)
    own = stack(
        [shares[0]] + [lax.ppermute(shares[step], "ulysses", turned[step]) for step in range(1, cores)]
    )
    waiting, _ = lax.optimization_barrier((query_int, own))
    queries = [query_int] + [lax.ppermute(waiting, "ulysses", turned[step]) for step in range(1, cores)]
    words = [bits(slashes, 0)] + [bits(verticals, low) for low in range(0, blocks, 32)]
    table = jnp.stack(words, axis=1).astype(jnp.int32)
    key_scales = jnp.pad(key_scale, ((0, 0), (0, query_scale.shape[1] - groups)))
    scales = jnp.concatenate([query_scale, key_scales], axis=0).astype(F32)

    climb = [(s, (s + pair) % spans) for s in range(spans)]
    up = [(s, s + pair) for s in range(spans - pair)]
    swap = [(s, s ^ 1) for s in range(spans)]
    turns = tuple(range(cores - 1, -1, -1))
    climbed, crossed, state = own, None, None
    steps = lines + (pair == 2)
    for step in range(steps):
        last = step + 1 == steps
        sent, arrived = climbed, crossed
        climbed = lax.ppermute(sent, "blk", up if step > 1 else climb) if step + 1 < lines else None
        crossed = lax.ppermute(sent, "blk", swap) if pair == 2 and sent is not None else None
        units, arrays = [], []
        if sent is not None:
            units.append((step, False))
            arrays.append(sent)
        if arrived is not None:
            units.append((step - 1, True))
            arrays.append(arrived)
        run = functools.partial(attend_chunk, sizes, table, scales, queries, tuple(units), arrays, state)
        if not last:
            state = run(turns, False)
            state, crossed, climbed = lax.optimization_barrier((state, crossed, climbed))
    if cores == 1:
        return run(turns, True)[0]
    others = run(turns[:-1], True)
    out = run(turns[-1:], True)[0]
    arrived = [
        lax.ppermute(one, "ulysses", back[turn]) for turn, one in sorted(zip(turns[:-1], others), key=lambda x: x[0])
    ]
    return join(cores, out, arrived)


def solution(mesh):
    rows = P(("group", "blk", "ulysses"), None)
    in_specs = (rows, rows, rows, P(("group", "blk"), None), P("group", None), P("group", None), P("group", None))
    run = functools.partial(local, mesh.shape["blk"], mesh.shape["ulysses"])
    return jax.shard_map(run, mesh=mesh, in_specs=in_specs, out_specs=rows, check_vma=False)
```
